32 devices in a mesh: dp: 16 (over z, y, core), seq: 2 (over x).
Axes of the slice: x: 2, y: 2, z: 4, core: 2. Of those that a mesh axis runs over, the one named last changes fastest.
Arguments:
- tokens: bfloat16 [32768, 768], P(('dp', 'seq')), may hold values from -8 to 8
- gain_attn: bfloat16 [768], P('dp'), may hold values from 0.25 to 1.75
- w_qkv: bfloat16 [768, 2304], P('dp'), may hold values from -0.3125 to 0.3125
- w_out: bfloat16 [768, 768], P('dp'), may hold values from -1.25 to 1.25
- gain_mlp: bfloat16 [768], P('dp'), may hold values from 0.25 to 1.75
- w_in: bfloat16 [768, 2304], P('dp'), may hold values from -0.21875 to 0.21875
- w_down: bfloat16 [1152, 768], P('dp'), may hold values from -0.1875 to 0.1875
- d_out: bfloat16 [32768, 768], P(('dp', 'seq')), may hold values from -6 to 6
Outputs:
- mixed: bfloat16 [32768, 768], P(('dp', 'seq'))
- grad_tokens: float32 [32768, 768], P(('dp', 'seq'))
- grad_gain_attn: float32 [768], P('dp')
- grad_w_qkv: float32 [768, 2304], P('dp')
- grad_w_out: float32 [768, 768], P('dp')
- grad_gain_mlp: float32 [768], P('dp')
- grad_w_in: float32 [768, 2304], P('dp')
- grad_w_down: float32 [1152, 768], P('dp')
The draws below stay inside these ranges and needn't reach their ends.
All inputs are finite; a program needn't handle non-finite values.
Results may differ from the reference program's by a relative error of at most 0.017.
Values may be sent and summed in bfloat16 or wider, within the bound.
A program may use at most 256 MiB of HBM per device.

```python
import jax
import jax.numpy as jnp
from jax import lax

D = 768
HEADS = 12
HEAD_DIM = 64
FF = 1152
LENGTH = 2048
TOKENS = 32768


def raised(entries, key, source, target, blocks, factor):
    def block_of(axis_at):
        return (jnp.arange(entries.shape[axis_at]) // (entries.shape[axis_at] // blocks)).reshape((-1,) + (1,) * (entries.ndim - 1 - axis_at))

    first = jax.random.permutation(key, blocks)[block_of(target)]
    other_side = (block_of(target) + blocks // 2) % blocks
    return jnp.where((block_of(source) == first) | (block_of(source) == other_side), factor * entries, entries)


def block_levels(own_key, shape, cuts, low, largest):
    gain, own = 1.0, jax.random.fold_in(own_key, 6)
    for dim, parts in cuts:
        steps = jnp.exp(jax.random.uniform(jax.random.fold_in(own, dim), (parts,), jnp.float32, low / len(cuts), largest / len(cuts)))
        gain = gain * jnp.repeat(steps, shape[dim] // parts).reshape([-1 if axis == dim else 1 for axis in range(len(shape))])
    return gain


def bell_draw(key, dims, scale, most, pieces=(), held_as=jnp.bfloat16):
    values = scale * jax.random.normal(key, dims, jnp.float32)
    if pieces:
        values = values * block_levels(key, dims, pieces, -0.22, 0.18)
    return jnp.clip(values, -most, most).astype(held_as)


def bell_draw_with(own_key, extent, deviation, limit, pieces, heavy, kind=jnp.bfloat16):
    drawn = deviation * jax.random.normal(own_key, extent, jnp.float32)
    if pieces:
        drawn = drawn * block_levels(own_key, extent, pieces, -0.22, 0.18)
    return jnp.clip(raised(drawn, jax.random.fold_in(own_key, 3), *heavy), -limit, limit).astype(kind)


def setup_inputs(seed: int = 0) -> dict:
    key_of = jax.random.split(jax.random.key(seed), 9)
    tokens = bell_draw_with(key_of[0], (TOKENS, D), 1.0, 8.0, ((0, 32),), (0, 1, 32, 2.75))
    gain_attn = jnp.clip(1.0 + 0.15 * jax.random.normal(key_of[1], (D,), jnp.float32), 0.25, 1.75).astype(jnp.bfloat16)
    w_qkv = bell_draw(key_of[2], (D, 3 * D), (D // 2) ** -0.5, 0.3125, ((0, 16),))
    w_out = bell_draw(key_of[3], (D, D), (max(1, D // 32)) ** -0.5, 1.25, ((0, 16),))
    gain_mlp = jnp.clip(1.0 + 0.15 * jax.random.normal(key_of[4], (D,), jnp.float32), 0.25, 1.75).astype(jnp.bfloat16)
    w_in = bell_draw(key_of[5], (D, 2 * FF), D ** -0.5, 0.21875, ((0, 16),))
    w_down = bell_draw(key_of[6], (FF, D), FF ** -0.5, 0.1875, ((0, 16),))
    d_out = bell_draw(key_of[7], (TOKENS, D), 1.0, 6.0, ((0, 32),))
    return dict(tokens=tokens, gain_attn=gain_attn, w_qkv=w_qkv, w_out=w_out, gain_mlp=gain_mlp, w_in=w_in, w_down=w_down, d_out=d_out)


eps = 1e-05
rope_base = 160000.0
highest = lax.Precision.HIGHEST

@jax.custom_vjp
def low(v):
    return lax.optimization_barrier(v.astype(jnp.bfloat16)).astype(jnp.float32)

@jax.custom_vjp
def low_back(v):
    return v

def low_keep(v):
    return (low(v), None)

def low_pass(kept, grad):
    return (grad,)

def back_keep(v):
    return (v, None)

def back_low(kept, grad):
    return (low(grad),)
low.defvjp(low_keep, low_pass)
low_back.defvjp(back_keep, back_low)

def normalize(values_in, gain_vec):
    centre = values_in - lax.optimization_barrier(jnp.mean(values_in, axis=-1, keepdims=True))
    spread = lax.optimization_barrier(jnp.mean(centre * centre, axis=-1, keepdims=True))
    return centre * lax.rsqrt(spread + eps) * gain_vec

def rotary_tables(positions):
    half_dim = HEAD_DIM // 2
    inverse = rope_base ** (-(jnp.arange(half_dim).astype(jnp.float32) * 2.0) / HEAD_DIM)
    phases = positions[:, None] * inverse[None, :]
    phases = jnp.concatenate([phases, phases], axis=-1)
    return (jnp.cos(phases), jnp.sin(phases))

def rotate(vectors, cos_table, sin_table):
    lower = vectors[..., :HEAD_DIM // 2]
    upper = vectors[..., HEAD_DIM // 2:]
    turned = jnp.concatenate([-upper, lower], axis=-1)
    return vectors * cos_table[:, None, :] + turned * sin_table[:, None, :]

def attend(queries, key_rows, value_rows):
    block_rows = min(512, LENGTH)
    q_blocks = queries.reshape(LENGTH // block_rows, block_rows, HEADS, HEAD_DIM)
    score_scale = HEAD_DIM ** (-0.5)

    def one_block(q_block):
        scores = low_back(jnp.einsum('qhd,khd->hqk', q_block, key_rows, precision=highest) * score_scale)
        weights = low(jax.nn.softmax(scores, axis=-1))
        return jnp.einsum('hqk,khd->qhd', weights, value_rows, precision=highest)
    return lax.map(jax.checkpoint(one_block), q_blocks).reshape(LENGTH, HEADS, HEAD_DIM)

def layer(inputs, gain_one, w_qkv, w_out, gain_two, w_in, w_down):
    groups = inputs.shape[0]
    cos_table, sin_table = rotary_tables(jnp.arange(LENGTH).astype(jnp.float32))
    normed_one = low(normalize(inputs, gain_one))
    projected = low_back(jnp.einsum('gtd,de->gte', normed_one, w_qkv, precision=highest))
    shaped = projected.reshape(groups, LENGTH, 3, HEADS, HEAD_DIM)
    queries = low(rotate(shaped[:, :, 0], cos_table, sin_table))
    key_rows = low(rotate(shaped[:, :, 1], cos_table, sin_table))
    value_rows = low(shaped[:, :, 2])
    context = jax.vmap(attend)(queries, key_rows, value_rows).reshape(groups, LENGTH, D)
    context = low(low_back(context))
    attended = low_back(jnp.einsum('gtd,de->gte', context, w_out, precision=highest))
    hidden = inputs + attended
    normed_two = low(normalize(hidden, gain_two))
    gate_up = low_back(jnp.einsum('gtd,df->gtf', normed_two, w_in, precision=highest))
    activated = low(jax.nn.gelu(gate_up[..., :FF], approximate=False) * gate_up[..., FF:])
    return hidden + jnp.einsum('gtf,fd->gtd', activated, w_down, precision=highest)

def reference(tokens, gain_attn, w_qkv, w_out, gain_mlp, w_in, w_down, d_out):
    params = tuple((weight.astype(jnp.float32) for weight in (gain_attn, w_qkv, w_out, gain_mlp, w_in, w_down)))
    groups = tokens.shape[0] // (2 * LENGTH)
    inputs = tokens.astype(jnp.float32).reshape(groups, 2, LENGTH, D)
    cotangents = d_out.astype(jnp.float32).reshape(groups, 2, LENGTH, D)

    def one_group(totals, pair):
        x_group, d_group = pair
        result, pullback = jax.vjp(layer, x_group, *params)
        grads = pullback(d_group)
        totals = tuple((total + grad for total, grad in zip(totals, grads[1:])))
        return (totals, (result.astype(jnp.bfloat16), grads[0]))
    start = tuple((jnp.zeros_like(weight) for weight in params))
    totals, (outputs, grad_inputs) = lax.scan(one_group, start, (inputs, cotangents))
    mixed = outputs.reshape(tokens.shape[0], D)
    grad_tokens = grad_inputs.reshape(tokens.shape[0], D)
    return (mixed, grad_tokens, totals[0], totals[1], totals[2], totals[3], totals[4], totals[5])
```

```python
import functools

import jax
import jax.numpy as jnp
from jax import lax
from jax.experimental import pallas as pl
from jax.experimental.pallas import tpu as pltpu
from jax.sharding import PartitionSpec as P

D = 768
HEADS = 12
HEAD_DIM = 64
FF = 1152
PAIR = 2 * HEAD_DIM
PAIRS = HEADS // 2

eps = 1e-05
rope_base = 160000.0
LIMIT = 56 * 1024 * 1024
BF = jnp.bfloat16
F32 = jnp.float32


def normalize_rows(values_in, gain_vec):
    centre = values_in - jnp.mean(values_in, axis=-1, keepdims=True)
    spread = jnp.mean(centre * centre, axis=-1, keepdims=True)
    inv_std = lax.rsqrt(spread + eps)
    unit_rows = centre * inv_std
    return (unit_rows * gain_vec, unit_rows, inv_std)


def normalize_back(grad_normed, gain_vec, unit_rows, inv_std):
    grad_unit = grad_normed * gain_vec
    return inv_std * (
        grad_unit
        - jnp.mean(grad_unit, axis=-1, keepdims=True)
        - unit_rows * jnp.mean(grad_unit * unit_rows, axis=-1, keepdims=True)
    )


def rotary_tables(positions):
    half_dim = HEAD_DIM // 2
    inverse = rope_base ** (-(jnp.arange(half_dim).astype(F32) * 2.0) / HEAD_DIM)
    phases = positions[:, None] * inverse[None, :]
    cos_half, sin_half = jnp.cos(phases), jnp.sin(phases)
    return (
        jnp.concatenate([cos_half] * 4, axis=-1),
        jnp.concatenate([-sin_half, sin_half] * 2, axis=-1),
    )


def turn(u, cos_table, sin_table):
    width = u.shape[-1]
    half = HEAD_DIM // 2
    lane = lax.broadcasted_iota(jnp.int32, u.shape, 1)
    from_right = pltpu.roll(u, width - half, 1)
    from_left = pltpu.roll(u, half, 1)
    other = jnp.where((lane & half) == 0, from_right, from_left)
    return u * cos_table + other * sin_table


def dot(a, b, a_dim, b_dim):
    return lax.dot_general(a, b, (((a_dim,), (b_dim,)), ((), ())), preferred_element_type=F32)


def project_kernel(turned_blocks, factor, act_ref, w_ref, cos_ref, sin_ref, out_ref):
    u = dot(act_ref[...], w_ref[...], 1, 0)
    wide = u.shape[-1] // PAIR

    @pl.when(pl.program_id(0) < turned_blocks)
    def _():
        cos_table = jnp.concatenate([cos_ref[...]] * wide, axis=-1)
        sin_table = jnp.concatenate([sin_ref[...]] * wide, axis=-1)
        out_ref[...] = turn(u, cos_table, sin_table).astype(BF) * jnp.array(factor, BF)

    @pl.when(pl.program_id(0) >= turned_blocks)
    def _():
        out_ref[...] = u.astype(BF)


def project(act, weight, cos_table, sin_table, first, columns, turned, factor):
    rows = act.shape[0]
    wide = 256
    return pl.pallas_call(
        functools.partial(project_kernel, turned // wide, factor),
        grid=(columns // wide,),
        in_specs=[
            pl.BlockSpec((rows, D), lambda c: (0, 0)),
            pl.BlockSpec((D, wide), lambda c: (0, first // wide + c)),
            pl.BlockSpec((rows, PAIR), lambda c: (0, 0)),
            pl.BlockSpec((rows, PAIR), lambda c: (0, 0)),
        ],
        out_specs=pl.BlockSpec((rows, wide), lambda c: (0, c)),
        out_shape=jax.ShapeDtypeStruct((rows, columns), BF),
        compiler_params=pltpu.CompilerParams(vmem_limit_bytes=LIMIT),
        cost_estimate=pl.CostEstimate(
            flops=2 * rows * D * columns, bytes_accessed=4 * rows * D, transcendentals=0
        ),
    )(act, weight, cos_table, sin_table)


def lanes_of(head, rows):
    lane = lax.broadcasted_iota(jnp.int32, (rows, PAIR), 1)
    return (lane < HEAD_DIM) if head == 0 else (lane >= HEAD_DIM)


def low_mask(head):
    return lanes_of(head, 1).astype(F32).astype(BF)


def forward_kernel(last, block, *refs):
    if last:
        q_ref, k_ref, v_ref, o_in, m_in, l_in, ctx_ref, lse_ref = refs
    else:
        q_ref, k_ref, v_ref, o_ref, m_ref, l_ref = refs
    keys = k_ref[...]
    masks = [low_mask(0), low_mask(1)]
    ones = jnp.ones((1, PAIR), BF)
    values = [v_ref[...] * mask + (ones - mask) for mask in masks]
    left = lanes_of(0, block)
    for start in range(0, q_ref.shape[0], block):
        rows = pl.ds(start, block)
        q_rows = q_ref[rows, :]
        tops, outs = [], []
        for head in range(2):
            scores = dot(q_rows * masks[head], keys, 1, 1)
            top = jnp.max(scores, axis=-1, keepdims=True)
            if last:
                top = jnp.maximum(top, m_in[rows, head * HEAD_DIM : head * HEAD_DIM + 1])
            tops.append(top)
            outs.append(dot(jnp.exp(scores - top).astype(BF), values[head], 1, 0))
        top = jnp.where(left, tops[0], tops[1])
        out = jnp.where(left, outs[0], outs[1])
        total = pltpu.roll(jnp.where(left, outs[1], outs[0]), HEAD_DIM, 1)
        if last:
            kept = jnp.exp(m_in[rows, :] - top)
            out = out + kept * o_in[rows, :]
            total = total + kept * l_in[rows, :]
            ctx_ref[rows, :] = (out / total).astype(BF)
            lse_ref[rows, :] = top + jnp.log(total)
        else:
            o_ref[rows, :] = out
            m_ref[rows, :] = top
            l_ref[rows, :] = total


def pair_spec(rows, shift=0):
    return pl.BlockSpec((rows, PAIR), lambda p: (0, p + shift))


def attend_cost(rows, products):
    return pl.CostEstimate(
        flops=2 * rows * rows * 2 * PAIR * HEADS * products,
        bytes_accessed=rows * D * 24,
        transcendentals=rows * rows * HEADS,
    )


def forward(queries, kv, carried):
    rows = queries.shape[0]
    last = carried is not None
    wide = jax.ShapeDtypeStruct((rows, D), F32)
    shapes = [jax.ShapeDtypeStruct((rows, D), BF), wide] if last else [wide, wide, wide]
    return pl.pallas_call(
        functools.partial(forward_kernel, last, 256),
        grid=(PAIRS,),
        in_specs=[pair_spec(rows), pair_spec(rows), pair_spec(rows, PAIRS)]
        + [pair_spec(rows)] * (3 if last else 0),
        out_specs=[pair_spec(rows)] * len(shapes),
        out_shape=shapes,
        compiler_params=pltpu.CompilerParams(vmem_limit_bytes=LIMIT),
        cost_estimate=attend_cost(rows, 2),
    )(queries, kv, kv, *(carried or ()))


def split_three(values_in):
    hi = values_in.astype(BF).astype(F32)
    rest = values_in - hi
    mid = rest.astype(BF).astype(F32)
    return hi, mid, rest - mid


def backward_kernel(last, block, *refs):
    if last:
        (q_ref, k_ref, v_ref, g_ref, ctx_ref, lse_ref, cos_ref, sin_ref, dq_in) = refs[:9]
        dq_ref, dk_ref, dv_ref, qa_ref, ga_ref, sum_ref = refs[9:]
    else:
        (q_ref, k_ref, v_ref, g_ref, ctx_ref, lse_ref, cos_ref, sin_ref) = refs[:8]
        dq_ref, dk_ref, dv_ref, qa_ref, ga_ref, sum_ref = refs[8:]
    count = q_ref.shape[0]
    queries = q_ref[...]
    grads = g_ref[...]
    product = grads.astype(F32) * ctx_ref[...].astype(F32)
    left = lanes_of(0, count)
    deltas = [
        jnp.sum(jnp.where(lanes_of(head, count), product, 0.0), axis=-1, keepdims=True)
        for head in range(2)
    ]
    log_parts = split_three(-pltpu.roll(lse_ref[...], HEAD_DIM, 1))
    delta_parts = split_three(-jnp.where(left, deltas[1], deltas[0]))
    lane = lax.broadcasted_iota(jnp.int32, (count, PAIR), 1)
    spot = lane & (HEAD_DIM - 1)

    def beside(own, base, parts):
        extra = jnp.where(spot == 0, parts[0], jnp.where(spot == 1, parts[1], parts[2]))
        extra = jnp.where(spot < 3, extra, 0.0)
        return jnp.where(own, base.astype(F32), extra).astype(BF)

    one_spot = ((lax.broadcasted_iota(jnp.int32, (1, PAIR), 1) & (HEAD_DIM - 1)) < 3).astype(F32)
    one_spot = one_spot.astype(BF)
    masks = [low_mask(0), low_mask(1)]
    ones = jnp.ones((1, PAIR), BF)
    for head in range(2):
        own = lanes_of(head, count)
        qa_ref[head] = beside(own, queries, log_parts)
        ga_ref[head] = beside(own, grads, delta_parts)
    left_block = lanes_of(0, block)
    for start in range(0, k_ref.shape[0], block):
        rows = pl.ds(start, block)
        k_rows, v_rows = k_ref[rows, :], v_ref[rows, :]
        dks, dvs = [], []
        for head in range(2):
            extra = (ones - masks[head]) * one_spot
            probs = jnp.exp(dot(k_rows * masks[head] + extra, qa_ref[head], 1, 1))
            centred = dot(v_rows * masks[head] + extra, ga_ref[head], 1, 1)
            dvs.append(dot(probs.astype(BF), grads, 1, 0))
            turned = (probs * centred).astype(BF)
            dks.append(dot(turned, queries, 1, 0))
            part = dot(turned, k_rows, 0, 0)
            if start == 0:
                sum_ref[head] = part
            else:
                sum_ref[head] += part
        dk = jnp.where(left_block, dks[0], dks[1])
        dk_ref[rows, :] = turn(dk, cos_ref[rows, :], -sin_ref[rows, :]).astype(BF)
        dv_ref[rows, :] = jnp.where(left_block, dvs[0], dvs[1]).astype(BF)
    dq = jnp.where(left, sum_ref[0], sum_ref[1]) * (HEAD_DIM**-0.5)
    if last:
        dq = dq + dq_in[...]
        dq_ref[...] = turn(dq, cos_ref[...], -sin_ref[...]).astype(BF)
    else:
        dq_ref[...] = dq


def backward(queries, kv, grads, ctx, lse, cos_table, sin_table, carried):
    rows = queries.shape[0]
    last = carried is not None
    low = jax.ShapeDtypeStruct((rows, D), BF)
    table = pl.BlockSpec((rows, PAIR), lambda p: (0, 0))
    args = [queries, kv, kv, grads, ctx, lse, cos_table, sin_table]
    specs = [pair_spec(rows), pair_spec(rows), pair_spec(rows, PAIRS)]
    specs += [pair_spec(rows)] * 3 + [table, table]
    if last:
        args.append(carried)
        specs.append(pair_spec(rows))
    return pl.pallas_call(
        functools.partial(backward_kernel, last, 256),
        grid=(PAIRS,),
        in_specs=specs,
        out_specs=[pair_spec(rows)] * 3,
        out_shape=[low if last else jax.ShapeDtypeStruct((rows, D), F32), low, low],
        scratch_shapes=[
            pltpu.VMEM((2, rows, PAIR), BF),
            pltpu.VMEM((2, rows, PAIR), BF),
            pltpu.VMEM((2, rows, PAIR), F32),
        ],
        compiler_params=pltpu.CompilerParams(vmem_limit_bytes=LIMIT),
        cost_estimate=attend_cost(rows, 5),
    )(*args)


def gated(gate_part, up_part):
    return jax.nn.gelu(gate_part, approximate=False) * up_part


def body(tokens, gain_attn, w_qkv, w_out, gain_mlp, w_in, w_down, d_out):
    ways = lax.axis_size("seq")
    tok_rows = tokens.shape[0]
    swap = [(i, (i + 1) % ways) for i in range(ways)]
    shard = gain_attn.shape[0]

    packed = jnp.concatenate(
        [w_qkv, gain_attn[:, None], gain_mlp[:, None], jnp.zeros((shard, PAIR - 2), BF)], axis=1
    )
    packed = lax.all_gather(packed, "dp", axis=0, tiled=True)
    full_out = lax.all_gather(w_out, "dp", axis=0, tiled=True)
    full_in = lax.all_gather(w_in, "dp", axis=0, tiled=True)
    full_down = lax.all_gather(w_down, "dp", axis=0, tiled=True)
    gain_one = packed[:, 3 * D].astype(F32)
    gain_two = packed[:, 3 * D + 1].astype(F32)

    here = lax.axis_index("seq")
    there = lax.rem(here + 1, ways)
    steps = jnp.arange(tok_rows)
    cos_here, sin_here = rotary_tables((here * tok_rows + steps).astype(F32))
    cos_there, sin_there = rotary_tables((there * tok_rows + steps).astype(F32))

    inputs = tokens.astype(F32)
    normed_one, unit_one, inv_one = normalize_rows(inputs, gain_one)
    act_one = normed_one.astype(BF)
    kv_here = project(act_one, packed, cos_here, sin_here, D, 2 * D, D, 1.0)
    kv_there = lax.ppermute(kv_here, "seq", swap)
    queries = project(act_one, packed, cos_here, sin_here, 0, D, D, HEAD_DIM**-0.5)
    partial = forward(queries, kv_here, None)
    ctx, lse = forward(queries, kv_there, partial)

    attended = jnp.dot(ctx, full_out, preferred_element_type=F32)
    hidden = inputs + attended
    normed_two, unit_two, inv_two = normalize_rows(hidden, gain_two)
    act_two = normed_two.astype(BF)
    gate_up = jnp.dot(act_two, full_in, preferred_element_type=F32)
    gated_value, gated_pull = jax.vjp(gated, gate_up[:, :FF], gate_up[:, FF:])
    activated = gated_value.astype(BF)
    mixed = (hidden + jnp.dot(activated, full_down, preferred_element_type=F32)).astype(BF)

    grad_out = d_out.astype(F32)
    grad_w_down = dot(activated, d_out, 0, 0)
    grad_act = dot(d_out, full_down, 1, 1)
    grad_gate, grad_up = gated_pull(grad_act)
    grad_gate_up = jnp.concatenate([grad_gate, grad_up], axis=1).astype(BF)
    grad_w_in = dot(act_two, grad_gate_up, 0, 0)
    grad_norm_two = dot(grad_gate_up, full_in, 1, 1)
    grad_hidden = grad_out + normalize_back(grad_norm_two, gain_two, unit_two, inv_two)
    grad_hidden_low = grad_hidden.astype(BF)
    grad_w_out = dot(ctx, grad_hidden_low, 0, 0)
    grad_ctx = dot(grad_hidden_low, full_out, 1, 1).astype(BF)

    dq_part, dk_far, dv_far = backward(
        queries, kv_there, grad_ctx, ctx, lse, cos_there, sin_there, None
    )
    dk_got = lax.ppermute(dk_far, "seq", swap)
    dv_got = lax.ppermute(dv_far, "seq", swap)
    dq, dk, dv = backward(queries, kv_here, grad_ctx, ctx, lse, cos_here, sin_here, dq_part)
    dk = (dk.astype(F32) + dk_got.astype(F32)).astype(BF)
    dv = (dv.astype(F32) + dv_got.astype(F32)).astype(BF)
    grad_proj = jnp.concatenate([dq, dk, dv], axis=1)

    grad_w_qkv = dot(act_one, grad_proj, 0, 0)
    full_qkv = packed[:, : 3 * D]
    grad_norm_one = dot(grad_proj, full_qkv, 1, 1)
    grad_tokens = grad_hidden + normalize_back(grad_norm_one, gain_one, unit_one, inv_one)

    def owned(grad):
        part = lax.psum_scatter(grad.astype(BF), "dp", scatter_dimension=0, tiled=True)
        other = lax.ppermute(part, "seq", swap)
        return part.astype(F32) + other.astype(F32)

    own_down, own_in, own_out, own_qkv = (
        owned(grad_w_down), owned(grad_w_in), owned(grad_w_out), owned(grad_w_qkv)
    )
    own_gain_one = jnp.sum(own_qkv * w_qkv.astype(F32), axis=1) / gain_attn.astype(F32)
    own_gain_two = jnp.sum(own_in * w_in.astype(F32), axis=1) / gain_mlp.astype(F32)
    return (
        mixed, grad_tokens, own_gain_one, own_qkv, own_out, own_gain_two, own_in, own_down
    )


def solution(mesh):
    in_specs = (
        P(("dp", "seq"), None),
        P("dp"),
        P("dp", None),
        P("dp", None),
        P("dp"),
        P("dp", None),
        P("dp", None),
        P(("dp", "seq"), None),
    )
    out_specs = (
        P(("dp", "seq"), None),
        P(("dp", "seq"), None),
        P("dp"),
        P("dp", None),
        P("dp", None),
        P("dp"),
        P("dp", None),
        P("dp", None),
    )
    return jax.shard_map(body, mesh=mesh, in_specs=in_specs, out_specs=out_specs, check_vma=False)
```

```python
import functools

import jax
import jax.numpy as jnp
from jax import lax
from jax.experimental import pallas as pl
from jax.experimental.pallas import tpu as pltpu
from jax.sharding import PartitionSpec as P

D = 768
HEADS = 12
HEAD_DIM = 64
FF = 1152
PAIR = 2 * HEAD_DIM
PAIRS = HEADS // 2
GROUP = 2
GROUPS = PAIRS // GROUP
WIDE = GROUP * PAIR

eps = 1e-05
rope_base = 160000.0
LIMIT = 56 * 1024 * 1024
BF = jnp.bfloat16
F32 = jnp.float32


def normalize_rows(values_in, gain_vec):
    centre = values_in - jnp.mean(values_in, axis=-1, keepdims=True)
    spread = jnp.mean(centre * centre, axis=-1, keepdims=True)
    inv_std = lax.rsqrt(spread + eps)
    unit_rows = centre * inv_std
    return (unit_rows * gain_vec, unit_rows, inv_std)


def normalize_back(grad_normed, gain_vec, unit_rows, inv_std):
    grad_unit = grad_normed * gain_vec
    return inv_std * (
        grad_unit
        - jnp.mean(grad_unit, axis=-1, keepdims=True)
        - unit_rows * jnp.mean(grad_unit * unit_rows, axis=-1, keepdims=True)
    )


def rotary_tables(positions):
    half_dim = HEAD_DIM // 2
    inverse = rope_base ** (-(jnp.arange(half_dim).astype(F32) * 2.0) / HEAD_DIM)
    phases = positions[:, None] * inverse[None, :]
    cos_half, sin_half = jnp.cos(phases), jnp.sin(phases)
    return (
        jnp.concatenate([cos_half] * 4, axis=-1),
        jnp.concatenate([-sin_half, sin_half] * 2, axis=-1),
    )


def turn(u, cos_table, sin_table):
    width = u.shape[-1]
    half = HEAD_DIM // 2
    lane = lax.broadcasted_iota(jnp.int32, u.shape, 1)
    from_right = pltpu.roll(u, width - half, 1)
    from_left = pltpu.roll(u, half, 1)
    other = jnp.where((lane & half) == 0, from_right, from_left)
    return u * cos_table + other * sin_table


def dot(a, b, a_dim, b_dim):
    return lax.dot_general(a, b, (((a_dim,), (b_dim,)), ((), ())), preferred_element_type=F32)


def project_kernel(turned_blocks, factor, act_ref, w_ref, cos_ref, sin_ref, out_ref):
    u = dot(act_ref[...], w_ref[...], 1, 0)
    wide = u.shape[-1] // PAIR

    @pl.when(pl.program_id(0) < turned_blocks)
    def _():
        cos_table = jnp.concatenate([cos_ref[...]] * wide, axis=-1)
        sin_table = jnp.concatenate([sin_ref[...]] * wide, axis=-1)
        out_ref[...] = turn(u, cos_table, sin_table).astype(BF) * jnp.array(factor, BF)

    @pl.when(pl.program_id(0) >= turned_blocks)
    def _():
        out_ref[...] = u.astype(BF)


def project(act, weight, cos_table, sin_table, first, step, count, turned, factor):
    rows = act.shape[0]
    columns = count * WIDE
    return pl.pallas_call(
        functools.partial(project_kernel, turned, factor),
        grid=(count,),
        in_specs=[
            pl.BlockSpec((rows, D), lambda c: (0, 0)),
            pl.BlockSpec((D, WIDE), lambda c: (0, first + step * c)),
            pl.BlockSpec((rows, PAIR), lambda c: (0, 0)),
            pl.BlockSpec((rows, PAIR), lambda c: (0, 0)),
        ],
        out_specs=pl.BlockSpec((rows, WIDE), lambda c: (0, c)),
        out_shape=jax.ShapeDtypeStruct((rows, columns), BF),
        compiler_params=pltpu.CompilerParams(vmem_limit_bytes=LIMIT),
        cost_estimate=pl.CostEstimate(
            flops=rows * D * PAIR, bytes_accessed=rows * PAIR, transcendentals=0
        ),
    )(act, weight, cos_table, sin_table)


def lanes_of(head, rows):
    lane = lax.broadcasted_iota(jnp.int32, (rows, PAIR), 1)
    return (lane < HEAD_DIM) if head == 0 else (lane >= HEAD_DIM)


def low_mask(head):
    return lanes_of(head, 1).astype(F32).astype(BF)


def forward_kernel(last, block, *refs):
    if last:
        q_ref, k_ref, v_ref, o_in, m_in, l_in, ctx_ref, lse_ref = refs
    else:
        q_ref, k_ref, v_ref, o_ref, m_ref, l_ref = refs
    keys = k_ref[...]
    masks = [low_mask(0), low_mask(1)]
    ones = jnp.ones((1, PAIR), BF)
    values = [v_ref[...] * mask + (ones - mask) for mask in masks]
    left = lanes_of(0, block)
    for start in range(0, q_ref.shape[0], block):
        rows = pl.ds(start, block)
        q_rows = q_ref[rows, :]
        tops, outs = [], []
        for head in range(2):
            scores = dot(q_rows * masks[head], keys, 1, 1)
            top = jnp.max(scores, axis=-1, keepdims=True)
            if last:
                top = jnp.maximum(top, m_in[rows, head * HEAD_DIM : head * HEAD_DIM + 1])
            tops.append(top)
            outs.append(dot(jnp.exp(scores - top).astype(BF), values[head], 1, 0))
        top = jnp.where(left, tops[0], tops[1])
        out = jnp.where(left, outs[0], outs[1])
        total = pltpu.roll(jnp.where(left, outs[1], outs[0]), HEAD_DIM, 1)
        if last:
            kept = jnp.exp(m_in[rows, :] - top)
            out = out + kept * o_in[rows, :]
            total = total + kept * l_in[rows, :]
            ctx_ref[rows, :] = (out / total).astype(BF)
            lse_ref[rows, :] = top + jnp.log(total)
        else:
            o_ref[rows, :] = out
            m_ref[rows, :] = top
            l_ref[rows, :] = total


def pair_spec(rows, shift=0):
    return pl.BlockSpec((rows, PAIR), lambda p: (0, p + shift))


def attend_cost(rows, products):
    return pl.CostEstimate(
        flops=rows * rows * PAIR * products, bytes_accessed=rows * PAIR, transcendentals=0
    )


def forward(group, queries, kv, carried):
    rows = queries.shape[0]
    last = carried is not None
    wide = jax.ShapeDtypeStruct((rows, WIDE), F32)
    shapes = [jax.ShapeDtypeStruct((rows, WIDE), BF), wide] if last else [wide, wide, wide]
    return pl.pallas_call(
        functools.partial(forward_kernel, last, 256),
        grid=(GROUP,),
        in_specs=[pair_spec(rows, group * GROUP), pair_spec(rows), pair_spec(rows, GROUP)]
        + [pair_spec(rows)] * (3 if last else 0),
        out_specs=[pair_spec(rows)] * len(shapes),
        out_shape=shapes,
        compiler_params=pltpu.CompilerParams(vmem_limit_bytes=LIMIT),
        cost_estimate=attend_cost(rows, 2),
    )(queries, kv, kv, *(carried or ()))


def split_three(values_in):
    hi = values_in.astype(BF).astype(F32)
    rest = values_in - hi
    mid = rest.astype(BF).astype(F32)
    return hi, mid, rest - mid


def backward_kernel(last, block, *refs):
    if last:
        (q_ref, k_ref, v_ref, g_ref, ctx_ref, lse_ref, cos_ref, sin_ref, dq_in) = refs[:9]
        dq_ref, dkv_ref, qa_ref, ga_ref, sum_ref = refs[9:]
    else:
        (q_ref, k_ref, v_ref, g_ref, ctx_ref, lse_ref, cos_ref, sin_ref) = refs[:8]
        dq_ref, dkv_ref, qa_ref, ga_ref, sum_ref = refs[8:]
    count = q_ref.shape[0]
    queries = q_ref[...]
    grads = g_ref[...]
    product = grads.astype(F32) * ctx_ref[...].astype(F32)
    left = lanes_of(0, count)
    deltas = [
        jnp.sum(jnp.where(lanes_of(head, count), product, 0.0), axis=-1, keepdims=True)
        for head in range(2)
    ]
    log_parts = split_three(-pltpu.roll(lse_ref[...], HEAD_DIM, 1))
    delta_parts = split_three(-jnp.where(left, deltas[1], deltas[0]))
    lane = lax.broadcasted_iota(jnp.int32, (count, PAIR), 1)
    spot = lane & (HEAD_DIM - 1)

    def beside(own, base, parts):
        extra = jnp.where(spot == 0, parts[0], jnp.where(spot == 1, parts[1], parts[2]))
        extra = jnp.where(spot < 3, extra, 0.0)
        return jnp.where(own, base.astype(F32), extra).astype(BF)

    one_spot = ((lax.broadcasted_iota(jnp.int32, (1, PAIR), 1) & (HEAD_DIM - 1)) < 3).astype(F32)
    one_spot = one_spot.astype(BF)
    masks = [low_mask(0), low_mask(1)]
    ones = jnp.ones((1, PAIR), BF)
    for head in range(2):
        own = lanes_of(head, count)
        qa_ref[head] = beside(own, queries, log_parts)
        ga_ref[head] = beside(own, grads, delta_parts)
    left_block = lanes_of(0, block)
    for start in range(0, k_ref.shape[0], block):
        rows = pl.ds(start, block)
        k_rows, v_rows = k_ref[rows, :], v_ref[rows, :]
        dks, dvs = [], []
        for head in range(2):
            extra = (ones - masks[head]) * one_spot
            probs = jnp.exp(dot(k_rows * masks[head] + extra, qa_ref[head], 1, 1))
            centred = dot(v_rows * masks[head] + extra, ga_ref[head], 1, 1)
            dvs.append(dot(probs.astype(BF), grads, 1, 0))
            turned = (probs * centred).astype(BF)
            dks.append(dot(turned, queries, 1, 0))
            part = dot(turned, k_rows, 0, 0)
            if start == 0:
                sum_ref[head] = part
            else:
                sum_ref[head] += part
        dk = jnp.where(left_block, dks[0], dks[1])
        dkv_ref[rows, :PAIR] = turn(dk, cos_ref[rows, :], -sin_ref[rows, :]).astype(BF)
        dkv_ref[rows, PAIR:] = jnp.where(left_block, dvs[0], dvs[1]).astype(BF)
    dq = jnp.where(left, sum_ref[0], sum_ref[1]) * (HEAD_DIM**-0.5)
    if last:
        dq = dq + dq_in[...]
        dq_ref[...] = turn(dq, cos_ref[...], -sin_ref[...]).astype(BF)
    else:
        dq_ref[...] = dq


def backward(group, queries, kv, grads, ctx, lse, cos_table, sin_table, carried):
    rows = queries.shape[0]
    last = carried is not None
    first = group * GROUP
    table = pl.BlockSpec((rows, PAIR), lambda p: (0, 0))
    args = [queries, kv, kv, grads, ctx, lse, cos_table, sin_table]
    specs = [pair_spec(rows, first), pair_spec(rows), pair_spec(rows, GROUP)]
    specs += [pair_spec(rows, first), pair_spec(rows), pair_spec(rows), table, table]
    if last:
        args.append(carried)
        specs.append(pair_spec(rows))
    return pl.pallas_call(
        functools.partial(backward_kernel, last, 256),
        grid=(GROUP,),
        in_specs=specs,
        out_specs=[pair_spec(rows), pl.BlockSpec((rows, 2 * PAIR), lambda p: (0, p))],
        out_shape=[
            jax.ShapeDtypeStruct((rows, WIDE), BF if last else F32),
            jax.ShapeDtypeStruct((rows, 2 * WIDE), BF),
        ],
        scratch_shapes=[
            pltpu.VMEM((2, rows, PAIR), BF),
            pltpu.VMEM((2, rows, PAIR), BF),
            pltpu.VMEM((2, rows, PAIR), F32),
        ],
        compiler_params=pltpu.CompilerParams(vmem_limit_bytes=LIMIT),
        cost_estimate=attend_cost(rows, 5),
    )(*args)


def after(value, earlier):
    return lax.optimization_barrier((value, earlier))[0]


def gated(gate_part, up_part):
    return jax.nn.gelu(gate_part, approximate=False) * up_part


def joined_grads(grad_w_in, grad_w_out, grad_w_down, shard):
    def by_owner(grad):
        return grad.astype(BF).reshape(D // shard, -1, D)

    parts = [by_owner(grad_w_in[:, start : start + D]) for start in range(0, 2 * FF, D)]
    parts += [by_owner(grad_w_out), by_owner(grad_w_down)]
    return jnp.concatenate(parts, axis=1).reshape(-1, D)


def body(tokens, gain_attn, w_qkv, w_out, gain_mlp, w_in, w_down, d_out):
    ways = lax.axis_size("seq")
    tok_rows = tokens.shape[0]
    swap = [(i, (i + 1) % ways) for i in range(ways)]
    shard = gain_attn.shape[0]

    packed = jnp.concatenate(
        [w_qkv, gain_attn[:, None], gain_mlp[:, None], jnp.zeros((shard, PAIR - 2), BF)], axis=1
    )
    packed = lax.all_gather(packed, "dp", axis=0, tiled=True)
    in_out = lax.all_gather(jnp.concatenate([w_in, w_out], axis=1), "dp", axis=0, tiled=True)
    full_in, full_out = in_out[:, : 2 * FF], in_out[:, 2 * FF :]
    full_down = lax.all_gather(w_down, "dp", axis=0, tiled=True)
    gain_one = packed[:, 3 * D].astype(F32)
    gain_two = packed[:, 3 * D + 1].astype(F32)

    here = lax.axis_index("seq")
    there = lax.rem(here + 1, ways)
    steps = jnp.arange(tok_rows)
    cos_here, sin_here = rotary_tables((here * tok_rows + steps).astype(F32))
    cos_there, sin_there = rotary_tables((there * tok_rows + steps).astype(F32))

    inputs = tokens.astype(F32)
    normed_one, unit_one, inv_one = normalize_rows(inputs, gain_one)
    act_one = normed_one.astype(BF)
    kv_here, kv_there = [], []
    for group in range(GROUPS):
        kv = project(act_one, packed, cos_here, sin_here, GROUPS + group, GROUPS, 2, 1, 1.0)
        kv_here.append(kv)
        kv_there.append(lax.ppermute(kv, "seq", swap))
    queries = project(
        act_one, packed, cos_here, sin_here, 0, 1, GROUPS, GROUPS, HEAD_DIM**-0.5
    )
    partial, both = [], []
    last_done = queries
    for group in range(GROUPS):
        partial.append(forward(group, after(queries, last_done), kv_here[group], None))
        last_done = partial[group][1]
    for group in range(GROUPS):
        both.append(
            forward(group, after(queries, last_done), kv_there[group], partial[group])
        )
        last_done = both[group][1]
    ctx_parts, lse_parts = [pair[0] for pair in both], [pair[1] for pair in both]
    ctx = jnp.concatenate(ctx_parts, axis=1)

    attended = jnp.dot(ctx, full_out, preferred_element_type=F32)
    hidden = inputs + attended
    normed_two, unit_two, inv_two = normalize_rows(hidden, gain_two)
    act_two = normed_two.astype(BF)
    gate_up = jnp.dot(act_two, full_in, preferred_element_type=F32)
    gated_value, gated_pull = jax.vjp(gated, gate_up[:, :FF], gate_up[:, FF:])
    activated = gated_value.astype(BF)
    mixed = (hidden + jnp.dot(activated, full_down, preferred_element_type=F32)).astype(BF)

    grad_out = d_out.astype(F32)
    grad_w_down = dot(activated, d_out, 0, 0)
    grad_act = dot(d_out, full_down, 1, 1)
    grad_gate, grad_up = gated_pull(grad_act)
    grad_gate_up = jnp.concatenate([grad_gate, grad_up], axis=1).astype(BF)
    grad_w_in = dot(act_two, grad_gate_up, 0, 0)
    grad_norm_two = dot(grad_gate_up, full_in, 1, 1)
    grad_hidden = grad_out + normalize_back(grad_norm_two, gain_two, unit_two, inv_two)
    grad_hidden_low = grad_hidden.astype(BF)
    grad_w_out = dot(ctx, grad_hidden_low, 0, 0)
    grad_ctx = dot(grad_hidden_low, full_out, 1, 1).astype(BF)

    joined = joined_grads(grad_w_in, grad_w_out, grad_w_down, shard)
    joined = lax.psum_scatter(joined, "dp", scatter_dimension=0, tiled=True)
    dq_parts, dkv_got = [], []
    last_done = grad_ctx
    for group in range(GROUPS):
        dq_part, dkv_far = backward(
            group, after(queries, last_done), kv_there[group], grad_ctx, ctx_parts[group], lse_parts[group],
            cos_there, sin_there, None,
        )
        dq_parts.append(dq_part)
        last_done = dq_part
        dkv_got.append(lax.ppermute(dkv_far, "seq", swap))
    dqs, dks, dvs = [], [], []
    for group in range(GROUPS):
        last_done = (last_done, dkv_got[group] if group + 1 < GROUPS else joined)
        dq, dkv = backward(
            group, after(queries, last_done), kv_here[group], grad_ctx, ctx_parts[group], lse_parts[group],
            cos_here, sin_here, dq_parts[group],
        )
        last_done = dq
        dkv = (dkv.astype(F32) + dkv_got[group].astype(F32)).astype(BF)
        dqs.append(dq)
        for start in range(0, 2 * WIDE, 2 * PAIR):
            dks.append(dkv[:, start : start + PAIR])
            dvs.append(dkv[:, start + PAIR : start + 2 * PAIR])
    grad_proj = jnp.concatenate(dqs + dks + dvs, axis=1)

    grad_w_qkv = dot(act_one, grad_proj, 0, 0)
    full_qkv = packed[:, : 3 * D]
    grad_norm_one = dot(grad_proj, full_qkv, 1, 1)
    grad_tokens = grad_hidden + normalize_back(grad_norm_one, gain_one, unit_one, inv_one)

    def owned(part):
        other = lax.ppermute(part, "seq", swap)
        return part.astype(F32) + other.astype(F32)

    grad_w_qkv = after(grad_w_qkv.astype(BF), joined)
    part_qkv = lax.psum_scatter(grad_w_qkv, "dp", scatter_dimension=0, tiled=True)
    own_joined = owned(joined)
    own_in = jnp.concatenate([own_joined[k * shard : (k + 1) * shard] for k in range(3)], axis=1)
    own_out = own_joined[3 * shard : 4 * shard]
    own_down = own_joined[4 * shard :]
    own_qkv = owned(part_qkv)
    own_gain_one = jnp.sum(own_qkv * w_qkv.astype(F32), axis=1) / gain_attn.astype(F32)
    own_gain_two = jnp.sum(own_in * w_in.astype(F32), axis=1) / gain_mlp.astype(F32)
    return (
        mixed, grad_tokens, own_gain_one, own_qkv, own_out, own_gain_two, own_in, own_down
    )


def solution(mesh):
    in_specs = (
        P(("dp", "seq"), None),
        P("dp"),
        P("dp", None),
        P("dp", None),
        P("dp"),
        P("dp", None),
        P("dp", None),
        P(("dp", "seq"), None),
    )
    out_specs = (
        P(("dp", "seq"), None),
        P(("dp", "seq"), None),
        P("dp"),
        P("dp", None),
        P("dp", None),
        P("dp"),
        P("dp", None),
        P("dp", None),
    )
    return jax.shard_map(body, mesh=mesh, in_specs=in_specs, out_specs=out_specs, check_vma=False)
```

```python
import functools

import jax
import jax.numpy as jnp
from jax import lax
from jax.experimental import pallas as pl
from jax.experimental.pallas import tpu as pltpu
from jax.sharding import PartitionSpec as P

D = 768
HEADS = 12
HEAD_DIM = 64
FF = 1152
PAIR = 2 * HEAD_DIM
PAIRS = HEADS // 2
GROUP = 3
GROUPS = PAIRS // GROUP
WIDE = GROUP * PAIR

eps = 1e-05
rope_base = 160000.0
LIMIT = 56 * 1024 * 1024
BF = jnp.bfloat16
F32 = jnp.float32


def normalize_rows(values_in, gain_vec):
    centre = values_in - jnp.mean(values_in, axis=-1, keepdims=True)
    spread = jnp.mean(centre * centre, axis=-1, keepdims=True)
    inv_std = lax.rsqrt(spread + eps)
    unit_rows = centre * inv_std
    return (unit_rows * gain_vec, unit_rows, inv_std)


def normalize_back(grad_normed, gain_vec, unit_rows, inv_std):
    grad_unit = grad_normed * gain_vec
    return inv_std * (
        grad_unit
        - jnp.mean(grad_unit, axis=-1, keepdims=True)
        - unit_rows * jnp.mean(grad_unit * unit_rows, axis=-1, keepdims=True)
    )


def rotary_tables(positions):
    half_dim = HEAD_DIM // 2
    inverse = rope_base ** (-(jnp.arange(half_dim).astype(F32) * 2.0) / HEAD_DIM)
    phases = positions[:, None] * inverse[None, :]
    cos_half, sin_half = jnp.cos(phases), jnp.sin(phases)
    return (
        jnp.concatenate([cos_half] * 4, axis=-1),
        jnp.concatenate([-sin_half, sin_half] * 2, axis=-1),
    )


def turn(u, cos_table, sin_table):
    width = u.shape[-1]
    half = HEAD_DIM // 2
    lane = lax.broadcasted_iota(jnp.int32, u.shape, 1)
    from_right = pltpu.roll(u, width - half, 1)
    from_left = pltpu.roll(u, half, 1)
    other = jnp.where((lane & half) == 0, from_right, from_left)
    return u * cos_table + other * sin_table


def dot(a, b, a_dim, b_dim):
    return lax.dot_general(a, b, (((a_dim,), (b_dim,)), ((), ())), preferred_element_type=F32)


def project_kernel(turned_blocks, factor, act_ref, w_ref, cos_ref, sin_ref, out_ref):
    u = dot(act_ref[...], w_ref[...], 1, 0)
    wide = u.shape[-1] // PAIR

    @pl.when(pl.program_id(0) < turned_blocks)
    def _():
        cos_table = jnp.concatenate([cos_ref[...]] * wide, axis=-1)
        sin_table = jnp.concatenate([sin_ref[...]] * wide, axis=-1)
        out_ref[...] = turn(u, cos_table, sin_table).astype(BF) * jnp.array(factor, BF)

    @pl.when(pl.program_id(0) >= turned_blocks)
    def _():
        out_ref[...] = u.astype(BF)


def project(act, weight, cos_table, sin_table, first, step, count, turned, factor):
    rows = act.shape[0]
    columns = count * WIDE
    return pl.pallas_call(
        functools.partial(project_kernel, turned, factor),
        grid=(count,),
        in_specs=[
            pl.BlockSpec((rows, D), lambda c: (0, 0)),
            pl.BlockSpec((D, WIDE), lambda c: (0, first + step * c)),
            pl.BlockSpec((rows, PAIR), lambda c: (0, 0)),
            pl.BlockSpec((rows, PAIR), lambda c: (0, 0)),
        ],
        out_specs=pl.BlockSpec((rows, WIDE), lambda c: (0, c)),
        out_shape=jax.ShapeDtypeStruct((rows, columns), BF),
        compiler_params=pltpu.CompilerParams(vmem_limit_bytes=LIMIT),
        cost_estimate=pl.CostEstimate(
            flops=rows * D * PAIR, bytes_accessed=rows * PAIR, transcendentals=0
        ),
    )(act, weight, cos_table, sin_table)


def lanes_of(head, rows):
    lane = lax.broadcasted_iota(jnp.int32, (rows, PAIR), 1)
    return (lane < HEAD_DIM) if head == 0 else (lane >= HEAD_DIM)


def low_mask(head):
    return lanes_of(head, 1).astype(F32).astype(BF)


def forward_kernel(last, block, *refs):
    if last:
        q_ref, k_ref, v_ref, o_in, m_in, l_in = refs[:6]
        ctx_ref, lse_ref = refs[-2:]
    else:
        q_ref, k_ref, v_ref, o_ref, m_ref, l_ref = refs
    keys = k_ref[...]
    masks = [low_mask(0), low_mask(1)]
    ones = jnp.ones((1, PAIR), BF)
    values = [v_ref[...] * mask + (ones - mask) for mask in masks]
    left = lanes_of(0, block)
    for start in range(0, q_ref.shape[0], block):
        rows = pl.ds(start, block)
        q_rows = q_ref[rows, :]
        tops, outs = [], []
        for head in range(2):
            scores = dot(q_rows * masks[head], keys, 1, 1)
            top = jnp.max(scores, axis=-1, keepdims=True)
            if last:
                top = jnp.maximum(top, m_in[rows, head * HEAD_DIM : head * HEAD_DIM + 1])
            tops.append(top)
            outs.append(dot(jnp.exp(scores - top).astype(BF), values[head], 1, 0))
        top = jnp.where(left, tops[0], tops[1])
        out = jnp.where(left, outs[0], outs[1])
        total = pltpu.roll(jnp.where(left, outs[1], outs[0]), HEAD_DIM, 1)
        if last:
            kept = jnp.exp(m_in[rows, :] - top)
            out = out + kept * o_in[rows, :]
            total = total + kept * l_in[rows, :]
            ctx_ref[rows, :] = (out / total).astype(BF)
            lse_ref[rows, :] = top + jnp.log(total)
        else:
            o_ref[rows, :] = out
            m_ref[rows, :] = top
            l_ref[rows, :] = total


def pair_spec(rows, shift=0):
    return pl.BlockSpec((rows, PAIR), lambda p: (0, p + shift))


def attend_cost(rows, products):
    return pl.CostEstimate(
        flops=rows * rows * PAIR * products, bytes_accessed=rows * PAIR, transcendentals=0
    )


def forward(group, queries, kv, carried, context=None):
    rows = queries.shape[0]
    last = carried is not None
    wide = jax.ShapeDtypeStruct((rows, WIDE), F32)
    shapes = [jax.ShapeDtypeStruct((rows, D), BF), wide] if last else [wide, wide, wide]
    outs = [pair_spec(rows)] * len(shapes)
    args, specs, aliases = [queries, kv, kv], [], {}
    if last:
        outs[0] = pair_spec(rows, group * GROUP)
        args += list(carried)
        if context is not None:
            aliases = {len(args): 0}
            args.append(context)
            specs = [pl.BlockSpec(memory_space=pl.ANY)]
    return pl.pallas_call(
        functools.partial(forward_kernel, last, 256),
        grid=(GROUP,),
        in_specs=[pair_spec(rows, group * GROUP), pair_spec(rows), pair_spec(rows, GROUP)]
        + [pair_spec(rows)] * (3 if last else 0)
        + specs,
        out_specs=outs,
        out_shape=shapes,
        input_output_aliases=aliases,
        compiler_params=pltpu.CompilerParams(vmem_limit_bytes=LIMIT),
        cost_estimate=attend_cost(rows, 2),
    )(*args)


def split_three(values_in):
    hi = values_in.astype(BF).astype(F32)
    rest = values_in - hi
    mid = rest.astype(BF).astype(F32)
    return hi, mid, rest - mid


def backward_kernel(last, block, *refs):
    if last:
        (q_ref, k_ref, v_ref, g_ref, ctx_ref, lse_ref, cos_ref, sin_ref, dq_in) = refs[:9]
        dq_ref, dkv_ref, qa_ref, ga_ref, sum_ref = refs[9:]
    else:
        (q_ref, k_ref, v_ref, g_ref, ctx_ref, lse_ref, cos_ref, sin_ref) = refs[:8]
        dq_ref, dkv_ref, qa_ref, ga_ref, sum_ref = refs[8:]
    count = q_ref.shape[0]
    queries = q_ref[...]
    grads = g_ref[...]
    product = grads.astype(F32) * ctx_ref[...].astype(F32)
    left = lanes_of(0, count)
    deltas = [
        jnp.sum(jnp.where(lanes_of(head, count), product, 0.0), axis=-1, keepdims=True)
        for head in range(2)
    ]
    log_parts = split_three(-pltpu.roll(lse_ref[...], HEAD_DIM, 1))
    delta_parts = split_three(-jnp.where(left, deltas[1], deltas[0]))
    lane = lax.broadcasted_iota(jnp.int32, (count, PAIR), 1)
    spot = lane & (HEAD_DIM - 1)

    def beside(own, base, parts):
        extra = jnp.where(spot == 0, parts[0], jnp.where(spot == 1, parts[1], parts[2]))
        extra = jnp.where(spot < 3, extra, 0.0)
        return jnp.where(own, base.astype(F32), extra).astype(BF)

    one_spot = ((lax.broadcasted_iota(jnp.int32, (1, PAIR), 1) & (HEAD_DIM - 1)) < 3).astype(F32)
    one_spot = one_spot.astype(BF)
    masks = [low_mask(0), low_mask(1)]
    ones = jnp.ones((1, PAIR), BF)
    for head in range(2):
        own = lanes_of(head, count)
        qa_ref[head] = beside(own, queries, log_parts)
        ga_ref[head] = beside(own, grads, delta_parts)
    left_block = lanes_of(0, block)
    for start in range(0, k_ref.shape[0], block):
        rows = pl.ds(start, block)
        k_rows, v_rows = k_ref[rows, :], v_ref[rows, :]
        dks, dvs = [], []
        for head in range(2):
            extra = (ones - masks[head]) * one_spot
            probs = jnp.exp(dot(k_rows * masks[head] + extra, qa_ref[head], 1, 1))
            centred = dot(v_rows * masks[head] + extra, ga_ref[head], 1, 1)
            dvs.append(dot(probs.astype(BF), grads, 1, 0))
            turned = (probs * centred).astype(BF)
            dks.append(dot(turned, queries, 1, 0))
            part = dot(turned, k_rows, 0, 0)
            if start == 0:
                sum_ref[head] = part
            else:
                sum_ref[head] += part
        dk = jnp.where(left_block, dks[0], dks[1])
        dkv_ref[rows, :PAIR] = turn(dk, cos_ref[rows, :], -sin_ref[rows, :]).astype(BF)
        dkv_ref[rows, PAIR:] = jnp.where(left_block, dvs[0], dvs[1]).astype(BF)
    dq = jnp.where(left, sum_ref[0], sum_ref[1]) * (HEAD_DIM**-0.5)
    if last:
        dq = dq + dq_in[...]
        dq_ref[...] = turn(dq, cos_ref[...], -sin_ref[...]).astype(BF)
    else:
        dq_ref[...] = dq


def backward(group, queries, kv, grads, ctx, lse, cos_table, sin_table, carried):
    rows = queries.shape[0]
    last = carried is not None
    first = group * GROUP
    table = pl.BlockSpec((rows, PAIR), lambda p: (0, 0))
    args = [queries, kv, kv, grads, ctx, lse, cos_table, sin_table]
    specs = [pair_spec(rows, first), pair_spec(rows), pair_spec(rows, GROUP)]
    specs += [pair_spec(rows, first), pair_spec(rows, first), pair_spec(rows), table, table]
    if last:
        args.append(carried)
        specs.append(pair_spec(rows))
    return pl.pallas_call(
        functools.partial(backward_kernel, last, 256),
        grid=(GROUP,),
        in_specs=specs,
        out_specs=[pair_spec(rows), pl.BlockSpec((rows, 2 * PAIR), lambda p: (0, p))],
        out_shape=[
            jax.ShapeDtypeStruct((rows, WIDE), BF if last else F32),
            jax.ShapeDtypeStruct((rows, 2 * WIDE), BF),
        ],
        scratch_shapes=[
            pltpu.VMEM((2, rows, PAIR), BF),
            pltpu.VMEM((2, rows, PAIR), BF),
            pltpu.VMEM((2, rows, PAIR), F32),
        ],
        compiler_params=pltpu.CompilerParams(vmem_limit_bytes=LIMIT),
        cost_estimate=attend_cost(rows, 5),
    )(*args)


def join_kernel(*refs):
    out_ref = refs[-1]
    for group in range(GROUPS):
        dq_ref, own_ref, got_ref = refs[group : 3 * GROUPS : GROUPS]
        out_ref[:, group * WIDE : (group + 1) * WIDE] = dq_ref[...]
        both = (own_ref[...].astype(F32) + got_ref[...].astype(F32)).astype(BF)
        for pair in range(GROUP):
            column = D + (group * GROUP + pair) * PAIR
            start = 2 * pair * PAIR
            out_ref[:, column : column + PAIR] = both[:, start : start + PAIR]
            out_ref[:, column + D : column + D + PAIR] = both[:, start + PAIR : start + 2 * PAIR]


def join(dqs, own, got):
    rows = dqs[0].shape[0]
    step = rows // 4
    narrow = pl.BlockSpec((step, WIDE), lambda r: (r, 0))
    double = pl.BlockSpec((step, 2 * WIDE), lambda r: (r, 0))
    return pl.pallas_call(
        join_kernel,
        grid=(rows // step,),
        in_specs=[narrow] * GROUPS + [double] * (2 * GROUPS),
        out_specs=pl.BlockSpec((step, 3 * D), lambda r: (r, 0)),
        out_shape=jax.ShapeDtypeStruct((rows, 3 * D), BF),
        compiler_params=pltpu.CompilerParams(vmem_limit_bytes=LIMIT),
    )(*dqs, *own, *got)


def after(value, earlier):
    return lax.optimization_barrier((value, earlier))[0]


def gated(gate_part, up_part):
    return jax.nn.gelu(gate_part, approximate=False) * up_part


def joined_grads(grad_w_in, grad_w_out, grad_w_down, shard):
    def by_owner(grad):
        return grad.astype(BF).reshape(D // shard, -1, D)

    parts = [by_owner(grad_w_in[:, start : start + D]) for start in range(0, 2 * FF, D)]
    parts += [by_owner(grad_w_out), by_owner(grad_w_down)]
    return jnp.concatenate(parts, axis=1).reshape(-1, D)


def body(tokens, gain_attn, w_qkv, w_out, gain_mlp, w_in, w_down, d_out):
    ways = lax.axis_size("seq")
    tok_rows = tokens.shape[0]
    swap = [(i, (i + 1) % ways) for i in range(ways)]
    shard = gain_attn.shape[0]

    packed = jnp.concatenate(
        [w_qkv, gain_attn[:, None], gain_mlp[:, None], jnp.zeros((shard, PAIR - 2), BF)], axis=1
    )
    packed = lax.all_gather(packed, "dp", axis=0, tiled=True)
    in_out = lax.all_gather(jnp.concatenate([w_in, w_out], axis=1), "dp", axis=0, tiled=True)
    full_in, full_out = in_out[:, : 2 * FF], in_out[:, 2 * FF :]
    full_down = lax.all_gather(w_down, "dp", axis=0, tiled=True)
    gain_one = packed[:, 3 * D].astype(F32)
    gain_two = packed[:, 3 * D + 1].astype(F32)

    here = lax.axis_index("seq")
    there = lax.rem(here + 1, ways)
    steps = jnp.arange(tok_rows)
    cos_here, sin_here = rotary_tables((here * tok_rows + steps).astype(F32))
    cos_there, sin_there = rotary_tables((there * tok_rows + steps).astype(F32))

    inputs = tokens.astype(F32)
    normed_one, unit_one, inv_one = normalize_rows(inputs, gain_one)
    act_one = normed_one.astype(BF)
    kv_here, kv_there = [], []
    for group in range(GROUPS):
        kv = project(act_one, packed, cos_here, sin_here, GROUPS + group, GROUPS, 2, 1, 1.0)
        kv_here.append(kv)
        kv_there.append(lax.ppermute(kv, "seq", swap))
    queries = project(
        act_one, packed, cos_here, sin_here, 0, 1, GROUPS, GROUPS, HEAD_DIM**-0.5
    )
    partial, lse_parts, ctx = [], [], None
    last_done = queries
    for group in range(GROUPS):
        partial.append(forward(group, after(queries, last_done), kv_here[group], None))
        last_done = partial[group][1]
    for group in range(GROUPS):
        ctx, lse = forward(
            group, after(queries, last_done), kv_there[group], partial[group], ctx
        )
        lse_parts.append(lse)
        last_done = lse

    attended = jnp.dot(ctx, full_out, preferred_element_type=F32)
    hidden = inputs + attended
    normed_two, unit_two, inv_two = normalize_rows(hidden, gain_two)
    act_two = normed_two.astype(BF)
    gate_up = jnp.dot(act_two, full_in, preferred_element_type=F32)
    gated_value, gated_pull = jax.vjp(gated, gate_up[:, :FF], gate_up[:, FF:])
    activated = gated_value.astype(BF)
    mixed = (hidden + jnp.dot(activated, full_down, preferred_element_type=F32)).astype(BF)

    grad_out = d_out.astype(F32)
    grad_w_down = dot(activated, d_out, 0, 0)
    grad_act = dot(d_out, full_down, 1, 1)
    grad_gate, grad_up = gated_pull(grad_act)
    grad_gate_up = jnp.concatenate([grad_gate, grad_up], axis=1).astype(BF)
    grad_w_in = dot(act_two, grad_gate_up, 0, 0)
    grad_norm_two = dot(grad_gate_up, full_in, 1, 1)
    grad_hidden = grad_out + normalize_back(grad_norm_two, gain_two, unit_two, inv_two)
    grad_hidden_low = grad_hidden.astype(BF)
    grad_w_out = dot(ctx, grad_hidden_low, 0, 0)
    grad_ctx = dot(grad_hidden_low, full_out, 1, 1).astype(BF)

    joined = joined_grads(grad_w_in, grad_w_out, grad_w_down, shard)
    joined = lax.psum_scatter(joined, "dp", scatter_dimension=0, tiled=True)
    dq_parts, dkv_got = [], []
    last_done = grad_ctx
    for group in range(GROUPS):
        dq_part, dkv_far = backward(
            group, after(queries, last_done), kv_there[group], grad_ctx, ctx, lse_parts[group],
            cos_there, sin_there, None,
        )
        dq_parts.append(dq_part)
        last_done = dq_part
        dkv_got.append(lax.ppermute(dkv_far, "seq", swap))
    dqs, dkvs = [], []
    for group in range(GROUPS):
        if group:
            last_done = (last_done, dkv_got[group - 1])
        dq, dkv = backward(
            group, after(queries, last_done), kv_here[group], grad_ctx, ctx, lse_parts[group],
            cos_here, sin_here, dq_parts[group],
        )
        last_done = dq
        dqs.append(dq)
        dkvs.append(dkv)
    grad_proj = join(dqs, dkvs, dkv_got)

    grad_w_qkv = dot(act_one, grad_proj, 0, 0)
    full_qkv = packed[:, : 3 * D]
    grad_norm_one = dot(grad_proj, full_qkv, 1, 1)
    grad_tokens = grad_hidden + normalize_back(grad_norm_one, gain_one, unit_one, inv_one)

    def owned(part):
        other = lax.ppermute(part, "seq", swap)
        return part.astype(F32) + other.astype(F32)

    grad_w_qkv = after(grad_w_qkv.astype(BF), joined)
    part_qkv = lax.psum_scatter(grad_w_qkv, "dp", scatter_dimension=0, tiled=True)
    own_joined = owned(joined)
    own_in = jnp.concatenate([own_joined[k * shard : (k + 1) * shard] for k in range(3)], axis=1)
    own_out = own_joined[3 * shard : 4 * shard]
    own_down = own_joined[4 * shard :]
    own_qkv = owned(part_qkv)
    own_gain_one = jnp.sum(own_qkv * w_qkv.astype(F32), axis=1) / gain_attn.astype(F32)
    own_gain_two = jnp.sum(own_in * w_in.astype(F32), axis=1) / gain_mlp.astype(F32)
    return (
        mixed, grad_tokens, own_gain_one, own_qkv, own_out, own_gain_two, own_in, own_down
    )


def solution(mesh):
    in_specs = (
        P(("dp", "seq"), None),
        P("dp"),
        P("dp", None),
        P("dp", None),
        P("dp"),
        P("dp", None),
        P("dp", None),
        P(("dp", "seq"), None),
    )
    out_specs = (
        P(("dp", "seq"), None),
        P(("dp", "seq"), None),
        P("dp"),
        P("dp", None),
        P("dp", None),
        P("dp"),
        P("dp", None),
        P("dp", None),
    )
    return jax.shard_map(body, mesh=mesh, in_specs=in_specs, out_specs=out_specs, check_vma=False)
```
